256 devices in a mesh: gx: 32 (over x_hi, z, core), gy: 8 (over x_lo, y).
Axes of the slice: x: 4 (x_hi: 2, x_lo: 2; x = x_hi * 2 + x_lo), y: 4, z: 8, core: 2. Of those that a mesh axis runs over, the one named last changes fastest.
Arguments:
- residual: float32 [4, 3, 16, 256, 2048], P(None, None, None, 'gx', 'gy'), may hold values from -6 to 6
- eps_inv: float32 [16, 256, 2048], P(None, 'gx', 'gy'), may hold values from 0.08 to 1
- region_ids: int32 [16, 256, 2048], P(None, 'gx', 'gy'), may hold values from 0 to 7
- source_mask: int32 [16, 256, 2048], P(None, 'gx', 'gy'), may hold values 0 or 1
- pole_a: float32 [8, 2], replicated, may hold values from 1.2 to 1.9602, as said below
- pole_b: float32 [8, 2], replicated, may hold values from -0.98 to -0.8
- pole_c: float32 [8, 2], replicated, may hold values from 0.1 to 0.4
- waveform: float32 [64, 4], replicated, may hold values from -4 to 4
- plan: int32 [4], replicated, may hold values from 0 to 63
Outputs:
- adjoint_e: float32 [4, 3, 16, 256, 2048], P(None, None, None, 'gx', 'gy')
- adjoint_h: float32 [4, 3, 16, 256, 2048], P(None, None, None, 'gx', 'gy')
The draws below stay inside these ranges and needn't reach their ends.
Inputs may be any that keep to these rules, and one draw needn't show every extreme that they name: For each region and pole, pole_a is at least 1.2 and below 0.99 * (1 - pole_b), so each pole's recurrence is stable.
All inputs are finite; a program needn't handle non-finite values. No bound on the sum of `source_mask` on one device may be relied on, other than what follows from the above.
Results may differ from the reference program's by a relative error of at most 0.00002.
Values sent between devices are 32-bit elements; how exact they have to be, the bound alone decides.
A program may use at most 64 MiB of HBM per device.

```python
import math
import jax
import jax.numpy as jnp
from jax import lax

NZ = 16
PORTS = 4
STEPS = 4
REGIONS = 8
REC = 64
NX = 256
NY = 2048


def pole_pair(key):
    key_b = jax.random.fold_in(key, 101)
    key_a = jax.random.fold_in(key, 202)
    coef_b = jax.random.uniform(key_b, (REGIONS, 2), jnp.float32, -0.98, -0.8)
    share = jax.random.uniform(key_a, (REGIONS, 2), jnp.float32, 0.0, 1.0)
    coef_a = 1.2 + share * (0.99 * (1.0 - coef_b) - 1.2)
    return (coef_a, coef_b)


def draw_pole_a(key, part):
    return pole_pair(key)[0]


def draw_pole_b(key, part):
    return pole_pair(key)[1]


def touch_ends(result, own_key, smallest, high):
    dims = result.shape
    index_at = [jax.random.randint(jax.random.fold_in(own_key, axis), (), 0, dims[axis]) for axis in range(len(dims))]
    result = result.at[tuple(index_at)].set(smallest)
    longest = dims.index(max(dims))
    index_at[longest] = (index_at[longest] + 1) % dims[longest]
    return result.at[tuple(index_at)].set(high)


def block_levels(own_key, extent, split, smallest, top_value):
    factor_of = 1.0
    for position, shards_of in split:
        steps = jax.random.uniform(jax.random.fold_in(jax.random.fold_in(own_key, 6), position), (shards_of,), jnp.float32, smallest / len(split), top_value / len(split))
        factor_of = factor_of * jnp.repeat(jnp.exp(steps), extent[position] // shards_of).reshape((-1,) + (1,) * (len(extent) - 1 - position))
    return factor_of


def centred(key, dims, deviation, limit, shards=(), kind=jnp.bfloat16):
    result = jax.random.normal(key, dims, jnp.float32) * deviation
    if len(shards) > 0:
        result = block_levels(key, dims, shards, -0.22, 0.18) * result
    return jnp.clip(result, min=-limit, max=limit).astype(kind)


def setup_inputs(seed: int = 0) -> dict:
    keys = jax.random.split(jax.random.key(seed), 10)
    residual = centred(keys[0], (PORTS, 3, NZ, NX, NY), 1.0, 6.0, ((3, 32), (4, 8)), jnp.float32)
    eps_inv = jnp.clip(jnp.exp(math.log(1.0) - 2.5257287 * jax.random.uniform(keys[1], (NZ, NX, NY), jnp.float32) ** block_levels(keys[1], (NZ, NX, NY), ((1, 32), (2, 8)), -0.2, 0.2)), 0.08, 1.0)
    region_ids = touch_ends(jax.random.randint(keys[2], (NZ, NX, NY), 0, REGIONS), jax.random.fold_in(keys[2], 1), 0, REGIONS - 1).astype(jnp.int32)
    source_mask = touch_ends((jax.random.randint(keys[3], (NZ, NX, NY), 0, 4) < 1).astype(jnp.int32), jax.random.fold_in(keys[3], 1), 0, 1)
    pole_a = draw_pole_a(jax.random.fold_in(keys[9], 71), 0)
    pole_b = draw_pole_b(jax.random.fold_in(keys[9], 71), 0)
    pole_c = jnp.clip(jax.random.uniform(keys[6], (REGIONS, 2), jnp.float32, 0.1, 0.4), 0.1, 0.4)
    waveform = centred(keys[7], (REC, PORTS), 1.0, 4.0, (), jnp.float32)
    plan = touch_ends(jax.random.randint(keys[8], (STEPS,), 0, REC), jax.random.fold_in(keys[8], 1), 0, REC - 1).astype(jnp.int32)
    return dict(residual=residual, eps_inv=eps_inv, region_ids=region_ids, source_mask=source_mask, pole_a=pole_a, pole_b=pole_b, pole_c=pole_c, waveform=waveform, plan=plan)


def upper_cell(field, axis):
    count = field.shape[axis]
    inner = lax.slice_in_dim(field, 1, count, axis=axis)
    zeros = jnp.zeros_like(lax.slice_in_dim(field, 0, 1, axis=axis))
    return jnp.concatenate([inner, zeros], axis)


def lower_cell(field, axis):
    count = field.shape[axis]
    inner = lax.slice_in_dim(field, 0, count - 1, axis=axis)
    zeros = jnp.zeros_like(lax.slice_in_dim(field, 0, 1, axis=axis))
    return jnp.concatenate([zeros, inner], axis)


def one_port(inputs):
    residual, amplitude, eps_inv, source_mask, coef_list = inputs
    mask_float = source_mask.astype(jnp.float32)
    zeros = jnp.zeros_like(eps_inv)
    elec = [zeros, zeros, zeros]
    magn = [zeros, zeros, zeros]
    state_u = [[zeros, zeros, zeros], [zeros, zeros, zeros]]
    state_v = [[zeros, zeros, zeros], [zeros, zeros, zeros]]
    for index_step in range(STEPS):
        elec = [elec[c] + mask_float * residual[c] * amplitude[index_step] for c in range(3)]
        elec_x, elec_y, elec_z = elec
        curl_x = (upper_cell(elec_z, 2) - elec_z) - (upper_cell(elec_y, 0) - elec_y)
        curl_y = (upper_cell(elec_x, 0) - elec_x) - (upper_cell(elec_z, 1) - elec_z)
        curl_z = (upper_cell(elec_y, 1) - elec_y) - (upper_cell(elec_x, 2) - elec_x)
        magn = [magn[0] - 0.5 * curl_x, magn[1] - 0.5 * curl_y, magn[2] - 0.5 * curl_z]
        magn_x, magn_y, magn_z = magn
        back_x = (magn_z - lower_cell(magn_z, 2)) - (magn_y - lower_cell(magn_y, 0))
        back_y = (magn_x - lower_cell(magn_x, 0)) - (magn_z - lower_cell(magn_z, 1))
        back_z = (magn_y - lower_cell(magn_y, 1)) - (magn_x - lower_cell(magn_x, 2))
        backs = [back_x, back_y, back_z]
        sectioned = [elec[c] + 0.5 * eps_inv * backs[c] for c in range(3)]
        change = [zeros, zeros, zeros]
        for pole in range(2):
            coef_a, coef_b, coef_c = coef_list[pole]
            new_u = [coef_a * state_u[pole][c] + state_v[pole][c] + coef_c * sectioned[c] for c in range(3)]
            state_v[pole] = [coef_b * state_u[pole][c] for c in range(3)]
            change = [change[c] + (new_u[c] - state_u[pole][c]) for c in range(3)]
            state_u[pole] = new_u
        elec = [sectioned[c] - eps_inv * change[c] for c in range(3)]
    return jnp.stack(elec, 0), jnp.stack(magn, 0)


def reference(residual, eps_inv, region_ids, source_mask, pole_a, pole_b, pole_c, waveform, plan):
    coef_list = [(pole_a[region_ids, pole], pole_b[region_ids, pole], pole_c[region_ids, pole]) for pole in range(2)]
    amplitudes = waveform[plan]

    def run_port(port_inputs):
        port_residual, port_amplitude = port_inputs
        return one_port((port_residual, port_amplitude, eps_inv, source_mask, coef_list))

    adjoint_e, adjoint_h = lax.map(run_port, (residual, jnp.transpose(amplitudes)))
    return adjoint_e, adjoint_h
```

```python
import functools

import jax
import jax.numpy as jnp
from jax import lax
from jax.experimental import pallas as pl
from jax.experimental.pallas import tpu as pltpu
from jax.sharding import PartitionSpec as P

MESH = pl.DeviceIdType.MESH
PORTS, NZ, ROWS, COLS = 4, 16, 8, 256
STEPS, REGIONS = 4, 8
LANES = 128
UNROLL = 4
OWN, HALO = 0, 1
FIELDS = 3 * PORTS + 2
NEIGHBOURS = [(1, 0), (-1, 0), (0, 1), (0, -1), (1, 1), (1, -1), (-1, 1), (-1, -1)]


def lane_tile(lt):
    return pl.ds(lt * LANES, LANES)


def kernel(
    residual, eps_inv, region_ids, source_mask, pole_a, pole_b, pole_c, waveform, plan,
    out_e, out_h,
    own_m, halo_m, ids, mask, consts, halo_consts, packed, recv_x, recv_y, recv_c,
    elec, magn, sect, coefs, strip_m, strip_e, strip_h, strip_s, strip_coefs,
    load_sem, send_sem, recv_sem,
):
    gx, gy = lax.axis_index("gx"), lax.axis_index("gy")
    size_x, size_y = lax.axis_size("gx"), lax.axis_size("gy")

    def there(dx, dy):
        x, y = gx + dx, gy + dy
        return (x >= 0) & (x < size_x) & (y >= 0) & (y < size_y)

    barrier = pltpu.get_barrier_semaphore()
    for dx, dy in NEIGHBOURS:
        @pl.when(there(dx, dy))
        def _(dx=dx, dy=dy):
            pl.semaphore_signal(
                barrier, inc=1, device_id=(gx + dx, gy + dy), device_id_type=MESH
            )

    loads = [
        pltpu.make_async_copy(source_mask, mask, load_sem.at[0]),
        pltpu.make_async_copy(residual, own_m, load_sem.at[1]),
        pltpu.make_async_copy(eps_inv, consts.at[0], load_sem.at[2]),
        pltpu.make_async_copy(region_ids, ids, load_sem.at[3]),
    ]
    for load in loads:
        load.start()

    lane = lax.broadcasted_iota(jnp.int32, (ROWS, LANES), 1)
    row = lax.broadcasted_iota(jnp.int32, (ROWS, LANES), 0)
    group = lax.rem(lane, 8)
    first_row, last_row = row == 0, row == ROWS - 1
    first_lane, last_lane = lane == 0, lane == LANES - 1
    first_z, last_z = lane < 8, lane >= LANES - 8
    left_cols = group < 4
    keep_low_x = (row < 4) | (gx > 0)
    keep_low_y = (group >= 4) | (gy > 0)
    zero = jnp.zeros((ROWS, LANES), jnp.float32)

    plane = jnp.zeros((4, COLS), jnp.float32)

    def clear_rows(lo):
        def body(z, carry):
            for p in range(PORTS):
                for c in range(3):
                    halo_m[p, c, z, lo:lo + 4, :] = plane
            for k in range(2):
                halo_consts[k, z, lo:lo + 4, :] = plane
            return carry

        lax.fori_loop(0, NZ, body, 0)
        recv_x[:, lo:lo + 4, :] = jnp.zeros((FIELDS, 4, LANES), jnp.float32)

    @pl.when(jnp.logical_not(there(1, 0)))
    def _():
        clear_rows(0)

    @pl.when(jnp.logical_not(there(-1, 0)))
    def _():
        clear_rows(4)

    for side, dy in ((0, -1), (1, 1)):
        @pl.when(jnp.logical_not(there(0, dy)))
        def _(side=side):
            recv_y[side] = jnp.zeros((FIELDS, ROWS, LANES), jnp.float32)

        for lo, dx in ((0, 1), (4, -1)):
            @pl.when(jnp.logical_not(there(dx, dy)))
            def _(side=side, lo=lo):
                recv_c[side, :, lo:lo + 4, :] = jnp.zeros((FIELDS, 4, LANES), jnp.float32)

    def clear_unsent(z, carry):
        for k in range(2):
            halo_consts[k, z, 3:5, :] = jnp.zeros((2, COLS), jnp.float32)
        return carry

    lax.fori_loop(0, NZ, clear_unsent, 0)
    for c in range(3):
        for rt in (OWN, HALO):
            elec[c, NZ, rt] = jnp.zeros((ROWS, COLS), jnp.float32)
            magn[c, 0, rt] = jnp.zeros((ROWS, COLS), jnp.float32)

    taps = [[], [], [], []]
    for region in range(REGIONS):
        total = [0.0, 0.0, 0.0, 0.0]
        for pole in range(2):
            a, b, c = pole_a[region, pole], pole_b[region, pole], pole_c[region, pole]
            u1 = c
            u2 = a * u1
            u3 = a * u2 + b * u1
            u4 = a * u3 + b * u2
            steps = (u1, u2 - u1, u3 - u2, u4 - u3)
            total = [total[j] + steps[j] for j in range(4)]
        for j in range(4):
            taps[j].append(total[j])

    def make_coefs(eps, region):
        hits = [region == jnp.float32(r) for r in range(REGIONS - 1)]
        result = [-0.25 * eps]
        for j in range(4):
            value = jnp.full((ROWS, LANES), taps[j][REGIONS - 1], jnp.float32)
            for r in range(REGIONS - 1):
                value = jnp.where(hits[r], taps[j][r], value)
            result.append(1.0 - eps * value if j == 0 else eps * value)
        return result

    for load in loads:
        load.wait()

    for f in range(FIELDS):
        packed[f] = zero

    def prepare(z, carry):
        at_z = (lane >= 8 * z) & (lane < 8 * z + 8)
        for lt in range(2):
            consts[1, z, :, lane_tile(lt)] = ids[z, :, lane_tile(lt)].astype(jnp.float32)
        weight = [mask[z, :, lane_tile(lt)].astype(jnp.float32) for lt in range(2)]
        for f in range(FIELDS):
            if f < 3 * PORTS:
                p, c = f // 3, f % 3
                tiles = []
                for lt in range(2):
                    value = own_m[p, c, z, :, lane_tile(lt)] * weight[lt]
                    own_m[p, c, z, :, lane_tile(lt)] = value
                    tiles.append(value)
            else:
                tiles = [consts[f - 3 * PORTS, z, :, lane_tile(lt)] for lt in range(2)]
            edge = jnp.where(lane < 4, tiles[0], tiles[1])
            packed[f] = jnp.where(at_z, pltpu.roll(edge, lax.rem(8 * z + 4, LANES), 1), packed[f])
        return carry

    lax.fori_loop(0, NZ, prepare, 0)

    peers = 0
    for dx, dy in NEIGHBOURS:
        peers = peers + jnp.where(there(dx, dy), 1, 0)
    pl.semaphore_wait(barrier, peers)

    def remote(index, src, dst, dx, dy):
        return pltpu.make_async_remote_copy(
            src_ref=src, dst_ref=dst, send_sem=send_sem.at[index], recv_sem=recv_sem.at[index],
            device_id=(gx + dx, gy + dy), device_id_type=MESH,
        )

    def rows_of(dx):
        return pl.ds(4, 4) if dx > 0 else pl.ds(0, 4)

    def port_copy(p, dx):
        side = 0 if dx > 0 else 1
        return remote(
            16 + 2 * p + side, own_m.at[p, :, :, rows_of(dx), :],
            halo_m.at[p, :, :, rows_of(dx), :], dx, 0,
        )

    edge_copies = []
    for dx in (1, -1):
        rows = pl.ds(5, 3) if dx > 0 else pl.ds(0, 3)
        edge_copies.append((dx, 0, remote(
            len(edge_copies), consts.at[:, :, rows, :], halo_consts.at[:, :, rows, :], dx, 0)))
    for dx, dy in NEIGHBOURS:
        if dy == 0:
            src, dst = packed.at[:, rows_of(dx), :], recv_x.at[:, rows_of(dx), :]
        elif dx == 0:
            src, dst = packed, recv_y.at[0 if dy > 0 else 1]
        else:
            src = packed.at[:, rows_of(dx), :]
            dst = recv_c.at[0 if dy > 0 else 1, :, rows_of(dx), :]
        edge_copies.append((dx, dy, remote(len(edge_copies), src, dst, dx, dy)))

    for dx, dy, copy in edge_copies:
        @pl.when(there(dx, dy))
        def _(copy=copy):
            copy.start()
    for p in range(PORTS):
        for dx in (1, -1):
            @pl.when(there(dx, 0))
            def _(p=p, dx=dx):
                port_copy(p, dx).start()

    def coef_rows(source, rt):
        def body(z, carry):
            for lt in range(2):
                values = make_coefs(source[0, z, :, lane_tile(lt)], source[1, z, :, lane_tile(lt)])
                for k in range(5):
                    coefs[k, z, rt, :, lane_tile(lt)] = values[k]
            return carry

        lax.fori_loop(0, NZ, body, 0)

    coef_rows(consts, OWN)
    for dx, dy, copy in edge_copies:
        @pl.when(there(-dx, -dy))
        def _(copy=copy):
            copy.wait_recv()
    coef_rows(halo_consts, HALO)
    for rt, source in ((OWN, recv_y), (HALO, recv_c)):
        for f in range(FIELDS - 2):
            strip_m[rt, f] = jnp.where(left_cols, source[0, f], source[1, f])
        eps, region = [
            jnp.where(left_cols, source[0, f], source[1, f]) for f in (FIELDS - 2, FIELDS - 1)
        ]
        values = make_coefs(eps, region)
        for k in range(5):
            strip_coefs[rt, k] = values[k]

    def up_row(values):
        rolled = [pltpu.roll(value, ROWS - 1, 0) for value in values]
        return [
            jnp.where(last_row, rolled[1 - rt], rolled[rt]) for rt in (OWN, HALO)
        ]

    def down_row(values):
        rolled = [pltpu.roll(value, 1, 0) for value in values]
        return [
            jnp.where(first_row, rolled[1 - rt], rolled[rt]) for rt in (OWN, HALO)
        ]

    def up_col(tiles, inserted):
        rolled = [pltpu.roll(tile, LANES - 1, 1) for tile in tiles]
        return [
            jnp.where(last_lane, rolled[1], rolled[0]),
            jnp.where(last_lane, inserted, rolled[1]),
        ]

    def down_col(tiles, inserted):
        rolled = [pltpu.roll(tile, 1, 1) for tile in tiles]
        return [
            jnp.where(first_lane, inserted, rolled[0]),
            jnp.where(first_lane, rolled[0], rolled[1]),
        ]

    both = (OWN, HALO)

    def strip_up_z(value):
        return jnp.where(last_z, 0.0, pltpu.roll(value, LANES - 8, 1))

    def strip_down_z(value):
        return jnp.where(first_z, 0.0, pltpu.roll(value, 8, 1))

    def strip_magnetic(s, gathered):
        ex, ey, ez = [[strip_e[rt, c] for rt in both] for c in range(3)]
        ey_up, ez_up = up_row(ey), up_row(ez)
        for rt in both:
            ex_next = jnp.where(group == 3, gathered[rt][0], pltpu.roll(ex[rt], LANES - 1, 1))
            ez_next = jnp.where(group == 3, gathered[rt][1], pltpu.roll(ez[rt], LANES - 1, 1))
            curls = (
                (ez_next - ez[rt]) - (strip_up_z(ey[rt]) - ey[rt]),
                (strip_up_z(ex[rt]) - ex[rt]) - (ez_up[rt] - ez[rt]),
                (ey_up[rt] - ey[rt]) - (ex_next - ex[rt]),
            )
            for c in range(3):
                value = curls[c] if s == 0 else strip_h[rt, c] + curls[c]
                if c != 1:
                    value = jnp.where(keep_low_y, value, 0.0)
                if c != 0 and rt == HALO:
                    value = jnp.where(keep_low_x, value, 0.0)
                strip_h[rt, c] = value

    def strip_electric(p, s, gathered, amplitude):
        hx, hy, hz = [[strip_h[rt, c] for rt in both] for c in range(3)]
        hy_down, hz_down = down_row(hy), down_row(hz)
        for rt in both:
            hx_prev = jnp.where(group == 4, gathered[rt][0], pltpu.roll(hx[rt], 1, 1))
            hz_prev = jnp.where(group == 4, gathered[rt][1], pltpu.roll(hz[rt], 1, 1))
            backs = (
                (hz[rt] - hz_prev) - (hy[rt] - strip_down_z(hy[rt])),
                (hx[rt] - strip_down_z(hx[rt])) - (hz[rt] - hz_down[rt]),
                (hy[rt] - hy_down[rt]) - (hx[rt] - hx_prev),
            )
            for c in range(3):
                value = strip_e[rt, c] + strip_coefs[rt, 0] * backs[c]
                strip_s[s, rt, c] = value
                new = strip_coefs[rt, 1] * value
                for j in range(1, s + 1):
                    new = new - strip_coefs[rt, 1 + j] * strip_s[s - j, rt, c]
                strip_e[rt, c] = new + strip_m[rt, 3 * p + c] * amplitude

    def cell_pass(p, s, amplitude):
        last = s == STEPS - 1

        def one_plane(z, gathered):
            (col_hx, col_hz), (col_ex, col_ez) = gathered
            el = [[[elec[c, z, rt, :, lane_tile(lt)] for lt in range(2)] for rt in both] for c in range(3)]
            up_z = [[[elec[c, z + 1, rt, :, lane_tile(lt)] for lt in range(2)] for rt in both] for c in range(2)]
            ex, ey, ez = el
            turn = lax.rem(251 - 8 * z, LANES)
            ey_xn = [up_row([ey[rt][lt] for rt in both]) for lt in range(2)]
            ez_xn = [up_row([ez[rt][lt] for rt in both]) for lt in range(2)]
            mags = [[[None] * 2 for _ in both] for _ in range(3)]
            for rt in both:
                ex_yn = up_col(ex[rt], pltpu.roll(strip_e[rt, 0], turn, 1))
                ez_yn = up_col(ez[rt], pltpu.roll(strip_e[rt, 2], turn, 1))
                for lt in range(2):
                    curls = (
                        (ez_yn[lt] - ez[rt][lt]) - (up_z[1][rt][lt] - ey[rt][lt]),
                        (up_z[0][rt][lt] - ex[rt][lt]) - (ez_xn[lt][rt] - ez[rt][lt]),
                        (ey_xn[lt][rt] - ey[rt][lt]) - (ex_yn[lt] - ex[rt][lt]),
                    )
                    for c in range(3):
                        if last and rt == HALO and c == 0:
                            continue
                        value = curls[c]
                        if s > 0:
                            value = magn[c, z + 1, rt, :, lane_tile(lt)] + value
                        if rt == HALO and c != 0:
                            value = jnp.where(keep_low_x, value, 0.0)
                        magn[c, z + 1, rt, :, lane_tile(lt)] = value
                        mags[c][rt][lt] = value
                        if last and rt == OWN:
                            out_h[p, c, z, :, lane_tile(lt)] = -0.5 * value
            hx, hy, hz = mags
            hy_xp = [down_row([hy[rt][lt] for rt in both]) for lt in range(2)]
            hz_xp = [down_row([hz[rt][lt] for rt in both]) for lt in range(2)]
            turn = lax.rem(253 - 8 * z, LANES)
            col_hx, col_hz, col_ex, col_ez = list(col_hx), list(col_hz), list(col_ex), list(col_ez)
            for rt in both:
                if last and rt == HALO:
                    continue
                hx_yp = down_col(hx[rt], pltpu.roll(strip_h[rt, 0], turn, 1))
                hz_yp = down_col(hz[rt], pltpu.roll(strip_h[rt, 2], turn, 1))
                if not last:
                    at = lane == 8 * z + 4
                    by = lax.rem(8 * z + 5, LANES)
                    col_hx[rt] = jnp.where(at, pltpu.roll(hx[rt][1], by, 1), col_hx[rt])
                    col_hz[rt] = jnp.where(at, pltpu.roll(hz[rt][1], by, 1), col_hz[rt])
                for lt in range(2):
                    hx_zp = magn[0, z, rt, :, lane_tile(lt)]
                    hy_zp = magn[1, z, rt, :, lane_tile(lt)]
                    backs = (
                        (hz[rt][lt] - hz_yp[lt]) - (hy[rt][lt] - hy_zp),
                        (hx[rt][lt] - hx_zp) - (hz[rt][lt] - hz_xp[lt][rt]),
                        (hy[rt][lt] - hy_xp[lt][rt]) - (hx[rt][lt] - hx_yp[lt]),
                    )
                    factors = [coefs[k, z, rt, :, lane_tile(lt)] for k in range(2 + s)]
                    source = own_m if rt == OWN else halo_m
                    for c in range(3):
                        value = el[c][rt][lt] + factors[0] * backs[c]
                        new = factors[1] * value
                        for j in range(1, s + 1):
                            new = new - factors[1 + j] * sect[s - j, c, z, rt, :, lane_tile(lt)]
                        if last:
                            out_e[p, c, z, :, lane_tile(lt)] = new
                            continue
                        new = new + source[p, c, z, :, lane_tile(lt)] * amplitude
                        sect[s, c, z, rt, :, lane_tile(lt)] = value
                        elec[c, z, rt, :, lane_tile(lt)] = new
                        if lt == 0 and c != 1:
                            at = lane == 8 * z + 3
                            rolled = pltpu.roll(new, lax.rem(8 * z + 3, LANES), 1)
                            if c == 0:
                                col_ex[rt] = jnp.where(at, rolled, col_ex[rt])
                            else:
                                col_ez[rt] = jnp.where(at, rolled, col_ez[rt])
            return ((tuple(col_hx), tuple(col_hz)), (tuple(col_ex), tuple(col_ez)))

        def body(block, gathered):
            for offset in range(UNROLL):
                gathered = one_plane(block * UNROLL + offset, gathered)
            return gathered

        start = (((zero, zero), (zero, zero)), ((zero, zero), (zero, zero)))
        if last:
            start = (((0, 0), (0, 0)), ((0, 0), (0, 0)))
        return lax.fori_loop(0, NZ // UNROLL, body, start)

    def port_body(p, carry):
        amplitude = [waveform[plan[s], p] for s in range(STEPS)]
        gathered = [
            [
                pltpu.roll(source[3 * p + c], LANES - 1, 1) * amplitude[0]
                for c in (0, 2)
            ]
            for source in (packed, recv_x)
        ]
        for rt in both:
            for c in range(3):
                strip_e[rt, c] = strip_m[rt, 3 * p + c] * amplitude[0]
        for dx in (1, -1):
            @pl.when(there(-dx, 0))
            def _(dx=dx):
                port_copy(p, dx).wait_recv()

        def first_source(z, inner):
            for rt, source in ((OWN, own_m), (HALO, halo_m)):
                for c in range(3):
                    for lt in range(2):
                        elec[c, z, rt, :, lane_tile(lt)] = source[p, c, z, :, lane_tile(lt)] * amplitude[0]
            return inner

        lax.fori_loop(0, NZ, first_source, 0)
        for s in range(STEPS):
            strip_magnetic(s, gathered)
            after = amplitude[min(s + 1, STEPS - 1)]
            (col_hx, col_hz), (col_ex, col_ez) = cell_pass(p, s, after)
            if s < STEPS - 1:
                strip_electric(p, s, [[col_hx[rt], col_hz[rt]] for rt in both], after)
                gathered = [[col_ex[rt], col_ez[rt]] for rt in both]
        return carry

    lax.fori_loop(0, PORTS, port_body, 0)

    for dx, dy, copy in edge_copies:
        @pl.when(there(dx, dy))
        def _(copy=copy):
            copy.wait_send()
    for p in range(PORTS):
        for dx in (1, -1):
            @pl.when(there(dx, 0))
            def _(p=p, dx=dx):
                port_copy(p, dx).wait_send()


def local(residual, eps_inv, region_ids, source_mask, pole_a, pole_b, pole_c, waveform, plan):
    hbm = pl.BlockSpec(memory_space=pl.ANY)
    smem = pl.BlockSpec(memory_space=pltpu.SMEM)
    vmem = pl.BlockSpec(memory_space=pltpu.VMEM)
    shape = (PORTS, 3, NZ, ROWS, COLS)
    f32 = jnp.float32
    return pl.pallas_call(
        kernel,
        out_shape=[jax.ShapeDtypeStruct(shape, f32)] * 2,
        in_specs=[hbm] * 4 + [smem] * 5,
        out_specs=[vmem] * 2,
        scratch_shapes=[
            pltpu.VMEM(shape, f32),
            pltpu.VMEM(shape, f32),
            pltpu.VMEM((NZ, ROWS, COLS), jnp.int32),
            pltpu.VMEM((NZ, ROWS, COLS), jnp.int32),
            pltpu.VMEM((2, NZ, ROWS, COLS), f32),
            pltpu.VMEM((2, NZ, ROWS, COLS), f32),
            pltpu.VMEM((FIELDS, ROWS, LANES), f32),
            pltpu.VMEM((FIELDS, ROWS, LANES), f32),
            pltpu.VMEM((2, FIELDS, ROWS, LANES), f32),
            pltpu.VMEM((2, FIELDS, ROWS, LANES), f32),
            pltpu.VMEM((3, NZ + 1, 2, ROWS, COLS), f32),
            pltpu.VMEM((3, NZ + 1, 2, ROWS, COLS), f32),
            pltpu.VMEM((STEPS - 1, 3, NZ, 2, ROWS, COLS), f32),
            pltpu.VMEM((5, NZ, 2, ROWS, COLS), f32),
            pltpu.VMEM((2, 3 * PORTS, ROWS, LANES), f32),
            pltpu.VMEM((2, 3, ROWS, LANES), f32),
            pltpu.VMEM((2, 3, ROWS, LANES), f32),
            pltpu.VMEM((STEPS - 1, 2, 3, ROWS, LANES), f32),
            pltpu.VMEM((2, 5, ROWS, LANES), f32),
            pltpu.SemaphoreType.DMA((4,)),
            pltpu.SemaphoreType.DMA((16 + 2 * PORTS,)),
            pltpu.SemaphoreType.DMA((16 + 2 * PORTS,)),
        ],
        compiler_params=pltpu.CompilerParams(
            collective_id=0, has_side_effects=True, vmem_limit_bytes=40 << 20
        ),
        cost_estimate=pl.CostEstimate(flops=60000000, bytes_accessed=5242880, transcendentals=0),
    )(residual, eps_inv, region_ids, source_mask, pole_a, pole_b, pole_c, waveform, plan)


def solution(mesh):
    cells = P(None, "gx", "gy")
    fields = P(None, None, None, "gx", "gy")
    return jax.shard_map(
        local,
        mesh=mesh,
        in_specs=(fields, cells, cells, cells, P(), P(), P(), P(), P()),
        out_specs=(fields, fields),
        check_vma=False,
    )
```

```python
import functools

import jax
import jax.numpy as jnp
from jax import lax
from jax.experimental import pallas as pl
from jax.experimental.pallas import tpu as pltpu
from jax.sharding import PartitionSpec as P

MESH = pl.DeviceIdType.MESH
PORTS, NZ, ROWS, COLS = 4, 16, 8, 256
STEPS, REGIONS = 4, 8
UNROLL = 8
LANES = 128
OWN, HALO = 0, 1
LEFT, RIGHT = 0, 1
FIELDS = 3 * PORTS + 2
NEIGHBOURS = [(1, 0), (-1, 0), (0, 1), (0, -1), (1, 1), (1, -1), (-1, 1), (-1, -1)]
EDGE_ORDER = NEIGHBOURS[4:] + NEIGHBOURS[2:4] + NEIGHBOURS[:2]


def lane_tile(lt):
    return pl.ds(lt * LANES, LANES)


def kernel(
    residual, eps_inv, region_ids, source_mask, pole_a_in, pole_b_in, pole_c_in, waveform_in, plan_in,
    out_e, out_h,
    pole_a, pole_b, pole_c, waveform, plan, own_m, halo_m, ids, mask, consts, halo_consts, packed, recv_x, recv_y, recv_c,
    elec_0, elec_1, magn_0, magn_1, sect_0, sect_1, sect_2, coefs, strip_m, strip_coefs, edge_e, edge_h, insert_e, insert_h,
    load_sem, send_sem, recv_sem,
):
    gx, gy = lax.axis_index("gx"), lax.axis_index("gy")
    elecs, magns, sects = (elec_0, elec_1), (magn_0, magn_1), (sect_0, sect_1, sect_2)
    size_x, size_y = lax.axis_size("gx"), lax.axis_size("gy")

    def there(dx, dy):
        x, y = gx + dx, gy + dy
        return (x >= 0) & (x < size_x) & (y >= 0) & (y < size_y)

    barrier = pltpu.get_barrier_semaphore()
    for dx, dy in NEIGHBOURS:
        @pl.when(there(dx, dy))
        def _(dx=dx, dy=dy):
            pl.semaphore_signal(
                barrier, inc=1, device_id=(gx + dx, gy + dy), device_id_type=MESH
            )

    loads = [
        pltpu.make_async_copy(source_mask, mask, load_sem.at[0]),
        pltpu.make_async_copy(residual, own_m.at[:, :, pl.ds(0, NZ)], load_sem.at[1]),
        pltpu.make_async_copy(eps_inv, consts.at[0], load_sem.at[2]),
        pltpu.make_async_copy(region_ids, ids, load_sem.at[3]),
    ]
    small = (
        (pole_a_in, pole_a), (pole_b_in, pole_b), (pole_c_in, pole_c),
        (waveform_in, waveform), (plan_in, plan),
    )
    small_loads = [
        pltpu.make_async_copy(source, target, load_sem.at[4 + index])
        for index, (source, target) in enumerate(small)
    ]
    loads = loads + small_loads
    for load in loads:
        load.start()

    lane = lax.broadcasted_iota(jnp.int32, (ROWS, LANES), 1)
    row = lax.broadcasted_iota(jnp.int32, (ROWS, LANES), 0)
    group = lax.rem(lane, 8)
    first_row, last_row = row == 0, row == ROWS - 1
    first_lane, last_lane = lane == 0, lane == LANES - 1
    first_z, last_z = lane < 8, lane >= LANES - 8
    left_cols = group < 4
    keep_low_x = (row < 4) | (gx > 0)
    keep_low_y = (group >= 4) | (gy > 0)
    zero = jnp.zeros((ROWS, LANES), jnp.float32)

    plane = jnp.zeros((4, COLS), jnp.float32)

    def clear_rows(lo):
        def body(z, carry):
            for p in range(PORTS):
                for c in range(3):
                    halo_m[p, c, z, lo:lo + 4, :] = plane
            for k in range(2):
                halo_consts[k, z, lo:lo + 4, :] = plane
            return carry

        lax.fori_loop(0, NZ, body, 0)
        recv_x[:, lo:lo + 4, :] = jnp.zeros((FIELDS, 4, LANES), jnp.float32)

    @pl.when(jnp.logical_not(there(1, 0)))
    def _():
        clear_rows(0)

    @pl.when(jnp.logical_not(there(-1, 0)))
    def _():
        clear_rows(4)

    for side, dy in ((0, -1), (1, 1)):
        @pl.when(jnp.logical_not(there(0, dy)))
        def _(side=side):
            recv_y[side] = jnp.zeros((FIELDS, ROWS, LANES), jnp.float32)

        for lo, dx in ((0, 1), (4, -1)):
            @pl.when(jnp.logical_not(there(dx, dy)))
            def _(side=side, lo=lo):
                recv_c[side, :, lo:lo + 4, :] = jnp.zeros((FIELDS, 4, LANES), jnp.float32)

    def clear_unsent(z, carry):
        for k in range(2):
            halo_consts[k, z, 3:5, :] = jnp.zeros((2, COLS), jnp.float32)
        return carry

    lax.fori_loop(0, NZ, clear_unsent, 0)
    for p in range(PORTS):
        for c in range(2):
            own_m[p, c, NZ] = jnp.zeros((ROWS, COLS), jnp.float32)
            halo_m[p, c, NZ] = jnp.zeros((ROWS, COLS), jnp.float32)
    for ref in elecs:
        for c in range(2):
            for rt in (OWN, HALO):
                ref[c, NZ, rt] = jnp.zeros((ROWS, COLS), jnp.float32)

    for load in small_loads:
        load.wait()

    taps = [[], [], [], []]
    for region in range(REGIONS):
        total = [0.0, 0.0, 0.0, 0.0]
        for pole in range(2):
            a, b, c = pole_a[pole, region], pole_b[pole, region], pole_c[pole, region]
            u1 = c
            u2 = a * u1
            u3 = a * u2 + b * u1
            u4 = a * u3 + b * u2
            steps = (u1, u2 - u1, u3 - u2, u4 - u3)
            total = [total[j] + steps[j] for j in range(4)]
        for j in range(4):
            taps[j].append(total[j])

    def make_coefs(eps, region):
        hits = [region == jnp.float32(r) for r in range(REGIONS - 1)]
        result = [-0.25 * eps]
        for j in range(4):
            value = jnp.full((ROWS, LANES), taps[j][REGIONS - 1], jnp.float32)
            for r in range(REGIONS - 1):
                value = jnp.where(hits[r], taps[j][r], value)
            result.append(1.0 - eps * value if j == 0 else eps * value)
        return result

    for load in loads[:4]:
        load.wait()

    for f in range(FIELDS):
        packed[f] = zero

    def prepare(z, carry):
        at_z = (lane >= 8 * z) & (lane < 8 * z + 8)
        for lt in range(2):
            consts[1, z, :, lane_tile(lt)] = ids[z, :, lane_tile(lt)].astype(jnp.float32)
        weight = [mask[z, :, lane_tile(lt)].astype(jnp.float32) for lt in range(2)]
        for f in range(FIELDS):
            if f < 3 * PORTS:
                p, c = f // 3, f % 3
                tiles = []
                for lt in range(2):
                    value = own_m[p, c, z, :, lane_tile(lt)] * weight[lt]
                    own_m[p, c, z, :, lane_tile(lt)] = value
                    tiles.append(value)
            else:
                tiles = [consts[f - 3 * PORTS, z, :, lane_tile(lt)] for lt in range(2)]
            edge = jnp.where(lane < 4, tiles[0], tiles[1])
            packed[f] = jnp.where(at_z, pltpu.roll(edge, lax.rem(8 * z + 4, LANES), 1), packed[f])
        return carry

    lax.fori_loop(0, NZ, prepare, 0)

    peers = 0
    for dx, dy in NEIGHBOURS:
        peers = peers + jnp.where(there(dx, dy), 1, 0)
    pl.semaphore_wait(barrier, peers)

    def remote(index, src, dst, dx, dy):
        return pltpu.make_async_remote_copy(
            src_ref=src, dst_ref=dst, send_sem=send_sem.at[index], recv_sem=recv_sem.at[index],
            device_id=(gx + dx, gy + dy), device_id_type=MESH,
        )

    def rows_of(dx):
        return pl.ds(4, 4) if dx > 0 else pl.ds(0, 4)

    def port_copy(p, dx):
        side = 0 if dx > 0 else 1
        return remote(
            16 + 2 * p + side, own_m.at[p, :, pl.ds(0, NZ), rows_of(dx), :],
            halo_m.at[p, :, pl.ds(0, NZ), rows_of(dx), :], dx, 0,
        )

    edge_copies = []
    for dx, dy in EDGE_ORDER:
        if dy == 0:
            src, dst = packed.at[:, rows_of(dx), :], recv_x.at[:, rows_of(dx), :]
        elif dx == 0:
            src, dst = packed, recv_y.at[0 if dy > 0 else 1]
        else:
            src = packed.at[:, rows_of(dx), :]
            dst = recv_c.at[0 if dy > 0 else 1, :, rows_of(dx), :]
        edge_copies.append((dx, dy, remote(len(edge_copies), src, dst, dx, dy)))
    for dx in (1, -1):
        rows = pl.ds(5, 3) if dx > 0 else pl.ds(0, 3)
        edge_copies.append((dx, 0, remote(
            len(edge_copies), consts.at[:, :, rows, :], halo_consts.at[:, :, rows, :], dx, 0)))

    for dx, dy, copy in edge_copies:
        @pl.when(there(dx, dy))
        def _(copy=copy):
            copy.start()

    def start_port(p):
        for dx in (1, -1):
            @pl.when(there(dx, 0))
            def _(dx=dx):
                port_copy(p, dx).start()

    def sent_port(p):
        for dx in (1, -1):
            @pl.when(there(dx, 0))
            def _(dx=dx):
                port_copy(p, dx).wait_send()

    start_port(0)

    def coef_rows(source, rt):
        def body(z, carry):
            for lt in range(2):
                values = make_coefs(source[0, z, :, lane_tile(lt)], source[1, z, :, lane_tile(lt)])
                for k in range(5):
                    coefs[k, z, rt, :, lane_tile(lt)] = values[k]
            return carry

        lax.fori_loop(0, NZ, body, 0)

    coef_rows(consts, OWN)
    for dx, dy, copy in edge_copies:
        @pl.when(there(-dx, -dy))
        def _(copy=copy):
            copy.wait_recv()
    sent_port(0)
    start_port(1)
    coef_rows(halo_consts, HALO)
    for rt, middle, sides in ((OWN, packed, recv_y), (HALO, recv_x, recv_c)):
        for side in (LEFT, RIGHT):
            def joined(f):
                if side == LEFT:
                    return jnp.where(left_cols, sides[0, f], middle[f])
                return jnp.where(left_cols, middle[f], sides[1, f])

            for f in range(FIELDS - 2):
                strip_m[side, rt, f] = joined(f)
            values = make_coefs(joined(FIELDS - 2), joined(FIELDS - 1))
            for k in range(5):
                strip_coefs[side, rt, k] = values[k]

    def up_row(values):
        rolled = [pltpu.roll(value, ROWS - 1, 0) for value in values]
        return [
            jnp.where(last_row, rolled[1 - rt], rolled[rt]) for rt in (OWN, HALO)
        ]

    def down_row(values):
        rolled = [pltpu.roll(value, 1, 0) for value in values]
        return [
            jnp.where(first_row, rolled[1 - rt], rolled[rt]) for rt in (OWN, HALO)
        ]

    def up_col(tiles, inserted):
        rolled = [pltpu.roll(tile, LANES - 1, 1) for tile in tiles]
        return [
            jnp.where(last_lane, rolled[1], rolled[0]),
            jnp.where(last_lane, inserted, rolled[1]),
        ]

    def up_col_first(tiles, inserted):
        return [
            pltpu.roll(jnp.where(first_lane, tiles[1], tiles[0]), LANES - 1, 1),
            pltpu.roll(jnp.where(first_lane, inserted, tiles[1]), LANES - 1, 1),
        ]

    def down_col(tiles, inserted):
        rolled = [pltpu.roll(tile, 1, 1) for tile in tiles]
        return [
            jnp.where(first_lane, inserted, rolled[0]),
            jnp.where(first_lane, rolled[0], rolled[1]),
        ]

    def down_col_last(tiles, inserted):
        return [
            pltpu.roll(jnp.where(last_lane, inserted, tiles[0]), 1, 1),
            pltpu.roll(jnp.where(last_lane, tiles[0], tiles[1]), 1, 1),
        ]

    both = (OWN, HALO)

    def strip_up_z(value):
        return jnp.where(last_z, 0.0, pltpu.roll(value, LANES - 8, 1))

    def strip_down_z(value):
        return jnp.where(first_z, 0.0, pltpu.roll(value, 8, 1))

    def strip_steps(p):
        amplitude = [waveform[p, plan[s]] for s in range(STEPS)]
        el = [
            [[strip_m[side, rt, 3 * p + c] * amplitude[0] for rt in both] for c in range(3)]
            for side in (LEFT, RIGHT)
        ]
        mags = [None, None]
        sects = [[], []]
        for s in range(STEPS):
            ex, ez = el[RIGHT][0], el[RIGHT][2]
            for rt in both:
                edge_e[p, s, rt] = jnp.where(group == 5, pltpu.roll(ex[rt], 1, 1), ez[rt])
            for side in (LEFT, RIGHT):
                if side == RIGHT and s == STEPS - 1:
                    continue
                ex, ey, ez = el[side]
                ey_up, ez_up = up_row(ey), up_row(ez)
                new = [[None, None] for _ in range(3)]
                for rt in both:
                    curls = (
                        (pltpu.roll(ez[rt], LANES - 1, 1) - ez[rt]) - (strip_up_z(ey[rt]) - ey[rt]),
                        (strip_up_z(ex[rt]) - ex[rt]) - (ez_up[rt] - ez[rt]),
                        (ey_up[rt] - ey[rt]) - (pltpu.roll(ex[rt], LANES - 1, 1) - ex[rt]),
                    )
                    for c in range(3):
                        value = curls[c] if s == 0 else mags[side][c][rt] + curls[c]
                        if c != 1 and side == LEFT:
                            value = jnp.where(keep_low_y, value, 0.0)
                        if c != 0 and rt == HALO:
                            value = jnp.where(keep_low_x, value, 0.0)
                        new[c][rt] = value
                mags[side] = new
                hx, hy, hz = new
                if side == LEFT:
                    for rt in both:
                        edge_h[p, s, rt] = jnp.where(group == 4, pltpu.roll(hz[rt], 1, 1), hx[rt])
                if s == STEPS - 1:
                    continue
                hy_down, hz_down = down_row(hy), down_row(hz)
                sect = [[None, None] for _ in range(3)]
                after = [[None, None] for _ in range(3)]
                for rt in both:
                    backs = (
                        (hz[rt] - pltpu.roll(hz[rt], 1, 1)) - (hy[rt] - strip_down_z(hy[rt])),
                        (hx[rt] - strip_down_z(hx[rt])) - (hz[rt] - hz_down[rt]),
                        (hy[rt] - hy_down[rt]) - (hx[rt] - pltpu.roll(hx[rt], 1, 1)),
                    )
                    for c in range(3):
                        value = el[side][c][rt] + strip_coefs[side, rt, 0] * backs[c]
                        sect[c][rt] = value
                        result = strip_coefs[side, rt, 1] * value
                        for j in range(1, s + 1):
                            result = result - strip_coefs[side, rt, 1 + j] * sects[side][s - j][c][rt]
                        after[c][rt] = result + strip_m[side, rt, 3 * p + c] * amplitude[s + 1]
                sects[side].append(sect)
                el[side] = after

    def cell_pass(p, s, amplitude):
        last = s == STEPS - 1
        elec_in, elec_out = elecs[s % 2], elecs[(s + 1) % 2]
        magn_in, magn_out = magns[(s + 1) % 2], magns[s % 2]
        sources = (own_m, halo_m)

        def read_elec(c, z):
            if s == 0:
                return [[sources[rt][p, c, z, :, lane_tile(lt)] * amplitude[0] for lt in range(2)] for rt in both]
            return [[elec_in[c, z, rt, :, lane_tile(lt)] for lt in range(2)] for rt in both]

        def one_plane(z, el, el_up, mag_down):
            ex, ey, ez = el
            ey_xn = [up_row([ey[rt][lt] for rt in both]) for lt in range(2)]
            ez_xn = [up_row([ez[rt][lt] for rt in both]) for lt in range(2)]
            mags = [[[None] * 2 for _ in both] for _ in range(3)]
            for rt in both:
                inserted = insert_e[p, s, rt, z]
                ex_yn = up_col_first(ex[rt], inserted)
                if not (last and rt == HALO):
                    ez_yn = up_col(ez[rt], inserted)
                for lt in range(2):
                    for c in range(3):
                        if last and rt == HALO and c == 0:
                            continue
                        if c == 0:
                            value = (ez_yn[lt] - ez[rt][lt]) - (el_up[1][rt][lt] - ey[rt][lt])
                        elif c == 1:
                            value = (el_up[0][rt][lt] - ex[rt][lt]) - (ez_xn[lt][rt] - ez[rt][lt])
                        else:
                            value = (ey_xn[lt][rt] - ey[rt][lt]) - (ex_yn[lt] - ex[rt][lt])
                        if s > 0:
                            value = magn_in[c, z, rt, :, lane_tile(lt)] + value
                        if rt == HALO and c != 0:
                            value = jnp.where(keep_low_x, value, 0.0)
                        if not last:
                            magn_out[c, z, rt, :, lane_tile(lt)] = value
                        elif rt == OWN:
                            out_h[p, c, z, :, lane_tile(lt)] = -0.5 * value
                        mags[c][rt][lt] = value
            hx, hy, hz = mags
            hy_xp = [down_row([hy[rt][lt] for rt in both]) for lt in range(2)]
            hz_xp = [down_row([hz[rt][lt] for rt in both]) for lt in range(2)]
            for rt in both:
                if last and rt == HALO:
                    continue
                inserted = insert_h[p, s, rt, z]
                hx_yp = down_col_last(hx[rt], inserted)
                hz_yp = down_col(hz[rt], inserted)
                for lt in range(2):
                    hx_zp, hy_zp = mag_down[0][rt][lt], mag_down[1][rt][lt]
                    backs = (
                        (hz[rt][lt] - hz_yp[lt]) - (hy[rt][lt] - hy_zp),
                        (hx[rt][lt] - hx_zp) - (hz[rt][lt] - hz_xp[lt][rt]),
                        (hy[rt][lt] - hy_xp[lt][rt]) - (hx[rt][lt] - hx_yp[lt]),
                    )
                    factors = [coefs[k, z, rt, :, lane_tile(lt)] for k in range(2 + s)]
                    for c in range(3):
                        value = el[c][rt][lt] + factors[0] * backs[c]
                        new = factors[1] * value
                        for j in range(1, s + 1):
                            new = new - factors[1 + j] * sects[s - j][c, z, rt, :, lane_tile(lt)]
                        if last:
                            out_e[p, c, z, :, lane_tile(lt)] = new
                            continue
                        new = new + sources[rt][p, c, z, :, lane_tile(lt)] * amplitude[s + 1]
                        sects[s][c, z, rt, :, lane_tile(lt)] = value
                        elec_out[c, z, rt, :, lane_tile(lt)] = new
            return mags

        nothing = (zero, zero)
        kept = (OWN,) if last else both

        def body(block, carry):
            mags = [[list(carry[c][rt]) if rt in kept else nothing for rt in both] for c in range(2)]
            first = block * UNROLL
            el = [read_elec(c, first) for c in range(3)]
            for offset in range(UNROLL):
                last_offset = offset == UNROLL - 1
                el_up = [read_elec(c, first + offset + 1) for c in range(2 if last_offset else 3)]
                mags = one_plane(first + offset, el, el_up, mags)
                el = el_up
            return tuple(tuple(tuple(mags[c][rt]) for rt in kept) for c in range(2))

        lax.fori_loop(0, NZ // UNROLL, body, ((nothing,) * len(kept),) * 2)

    def strips(block, carry):
        for offset in range(2):
            strip_steps(2 * block + offset)
        return carry

    def place(index, carry):
        p, s = index // STEPS, lax.rem(index, STEPS)
        for rt in both:
            value_e, value_h = edge_e[p, s, rt], edge_h[p, s, rt]
            for z in range(NZ):
                insert_e[p, s, rt, z] = pltpu.roll(value_e, (251 - 8 * z) % LANES, 1)
                insert_h[p, s, rt, z] = pltpu.roll(value_h, (252 - 8 * z) % LANES, 1)
        return carry

    lax.fori_loop(0, PORTS // 2, strips, 0)
    lax.fori_loop(0, PORTS * STEPS, place, 0)
    sent_port(1)
    start_port(2)

    def port_body(p, carry):
        amplitude = [waveform[p, plan[s]] for s in range(STEPS)]
        for dx in (1, -1):
            @pl.when(there(-dx, 0))
            def _(dx=dx):
                port_copy(p, dx).wait_recv()

        for s in range(STEPS):
            if s == 1:
                @pl.when(p == 0)
                def _():
                    sent_port(2)
                    start_port(3)

            cell_pass(p, s, amplitude)
        return carry

    lax.fori_loop(0, PORTS, port_body, 0)

    for dx, dy, copy in edge_copies:
        @pl.when(there(dx, dy))
        def _(copy=copy):
            copy.wait_send()
    sent_port(PORTS - 1)


def local(residual, eps_inv, region_ids, source_mask, pole_a, pole_b, pole_c, waveform, plan):
    hbm = pl.BlockSpec(memory_space=pl.ANY)
    vmem = pl.BlockSpec(memory_space=pltpu.VMEM)
    shape = (PORTS, 3, NZ, ROWS, COLS)
    f32 = jnp.float32
    return pl.pallas_call(
        kernel,
        out_shape=[jax.ShapeDtypeStruct(shape, f32)] * 2,
        in_specs=[hbm] * 9,
        out_specs=[vmem] * 2,
        scratch_shapes=[
            *[pltpu.SMEM((2, REGIONS), f32)] * 3,
            pltpu.SMEM((PORTS, waveform.shape[0]), f32),
            pltpu.SMEM((STEPS,), jnp.int32),
            *[pltpu.VMEM((PORTS, 3, NZ + 1, ROWS, COLS), f32)] * 2,
            pltpu.VMEM((NZ, ROWS, COLS), jnp.int32),
            pltpu.VMEM((NZ, ROWS, COLS), jnp.int32),
            pltpu.VMEM((2, NZ, ROWS, COLS), f32),
            pltpu.VMEM((2, NZ, ROWS, COLS), f32),
            pltpu.VMEM((FIELDS, ROWS, LANES), f32),
            pltpu.VMEM((FIELDS, ROWS, LANES), f32),
            pltpu.VMEM((2, FIELDS, ROWS, LANES), f32),
            pltpu.VMEM((2, FIELDS, ROWS, LANES), f32),
            *[pltpu.VMEM((3, NZ + 1, 2, ROWS, COLS), f32)] * 2,
            *[pltpu.VMEM((3, NZ, 2, ROWS, COLS), f32)] * 5,
            pltpu.VMEM((5, NZ, 2, ROWS, COLS), f32),
            pltpu.VMEM((2, 2, 3 * PORTS, ROWS, LANES), f32),
            pltpu.VMEM((2, 2, 5, ROWS, LANES), f32),
            *[pltpu.VMEM((PORTS, STEPS, 2, ROWS, LANES), f32)] * 2,
            *[pltpu.VMEM((PORTS, STEPS, 2, NZ, ROWS, LANES), f32)] * 2,
            pltpu.SemaphoreType.DMA((9,)),
            pltpu.SemaphoreType.DMA((16 + 2 * PORTS,)),
            pltpu.SemaphoreType.DMA((16 + 2 * PORTS,)),
        ],
        compiler_params=pltpu.CompilerParams(
            collective_id=0, has_side_effects=True, vmem_limit_bytes=40 << 20
        ),
        cost_estimate=pl.CostEstimate(flops=60000000, bytes_accessed=5242880, transcendentals=0),
    )(*[
        pltpu.with_memory_space_constraint(value, pltpu.HBM)
        for value in (
            residual, eps_inv, region_ids, source_mask, pole_a.T, pole_b.T, pole_c.T, waveform.T, plan
        )
    ])


def solution(mesh):
    cells = P(None, "gx", "gy")
    fields = P(None, None, None, "gx", "gy")
    return jax.shard_map(
        local,
        mesh=mesh,
        in_specs=(fields, cells, cells, cells, P(), P(), P(), P(), P()),
        out_specs=(fields, fields),
        check_vma=False,
    )
```

```python
import functools

import jax
import jax.numpy as jnp
from jax import lax
from jax.experimental import pallas as pl
from jax.experimental.pallas import tpu as pltpu
from jax.sharding import PartitionSpec as P

MESH = pl.DeviceIdType.MESH
PORTS, NZ, ROWS, COLS = 4, 16, 8, 256
STEPS, REGIONS = 4, 8
UNROLL = 8
LANES = 128
OWN, HALO = 0, 1
LEFT, RIGHT = 0, 1
FIELDS = 3 * PORTS + 2
NEIGHBOURS = [(1, 0), (-1, 0), (0, 1), (0, -1), (1, 1), (1, -1), (-1, 1), (-1, -1)]
EDGE_ORDER = NEIGHBOURS[4:] + NEIGHBOURS[2:4] + NEIGHBOURS[:2]


def lane_tile(lt):
    return pl.ds(lt * LANES, LANES)


def kernel(
    residual, eps_inv, region_ids, source_mask, pole_a_in, pole_b_in, pole_c_in, waveform_in, plan_in,
    out_e, out_h,
    pole_a, pole_b, pole_c, waveform, plan, own_m, halo_m, ids, mask, consts, halo_consts, packed, recv_x, recv_y, recv_c,
    elec_0, elec_1, magn_0, magn_1, sect_0, sect_1, sect_2, coefs, strip_m, strip_coefs, edge_e, edge_h, insert_e, insert_h,
    load_sem, send_sem, recv_sem,
):
    gx, gy = lax.axis_index("gx"), lax.axis_index("gy")
    elecs, magns, sects = (elec_0, elec_1), (magn_0, magn_1), (sect_0, sect_1, sect_2)
    size_x, size_y = lax.axis_size("gx"), lax.axis_size("gy")

    def there(dx, dy):
        x, y = gx + dx, gy + dy
        return (x >= 0) & (x < size_x) & (y >= 0) & (y < size_y)

    barrier = pltpu.get_barrier_semaphore()
    for dx, dy in NEIGHBOURS:
        @pl.when(there(dx, dy))
        def _(dx=dx, dy=dy):
            pl.semaphore_signal(
                barrier, inc=1, device_id=(gx + dx, gy + dy), device_id_type=MESH
            )

    loads = [
        pltpu.make_async_copy(source_mask, mask, load_sem.at[0]),
        pltpu.make_async_copy(residual, own_m.at[:, :, pl.ds(0, NZ)], load_sem.at[1]),
        pltpu.make_async_copy(eps_inv, consts.at[0], load_sem.at[2]),
        pltpu.make_async_copy(region_ids, ids, load_sem.at[3]),
    ]
    small = (
        (pole_a_in, pole_a), (pole_b_in, pole_b), (pole_c_in, pole_c),
        (waveform_in, waveform), (plan_in, plan),
    )
    small_loads = [
        pltpu.make_async_copy(source, target, load_sem.at[4 + index])
        for index, (source, target) in enumerate(small)
    ]
    loads = loads + small_loads
    for load in loads:
        load.start()

    lane = lax.broadcasted_iota(jnp.int32, (ROWS, LANES), 1)
    row = lax.broadcasted_iota(jnp.int32, (ROWS, LANES), 0)
    group = lax.rem(lane, 8)
    first_row, last_row = row == 0, row == ROWS - 1
    first_lane, last_lane = lane == 0, lane == LANES - 1
    first_z, last_z = lane < 8, lane >= LANES - 8
    left_cols = group < 4
    keep_low_x = (row < 4) | (gx > 0)
    keep_low_y = (group >= 4) | (gy > 0)
    zero = jnp.zeros((ROWS, LANES), jnp.float32)

    plane = jnp.zeros((4, COLS), jnp.float32)

    def clear_rows(lo):
        def body(z, carry):
            for p in range(PORTS):
                for c in range(3):
                    halo_m[p, c, z, lo:lo + 4, :] = plane
            for k in range(2):
                halo_consts[k, z, lo:lo + 4, :] = plane
            return carry

        lax.fori_loop(0, NZ, body, 0)
        recv_x[:, lo:lo + 4, :] = jnp.zeros((FIELDS, 4, LANES), jnp.float32)

    @pl.when(jnp.logical_not(there(1, 0)))
    def _():
        clear_rows(0)

    @pl.when(jnp.logical_not(there(-1, 0)))
    def _():
        clear_rows(4)

    for side, dy in ((0, -1), (1, 1)):
        @pl.when(jnp.logical_not(there(0, dy)))
        def _(side=side):
            recv_y[side] = jnp.zeros((FIELDS, ROWS, LANES), jnp.float32)

        for lo, dx in ((0, 1), (4, -1)):
            @pl.when(jnp.logical_not(there(dx, dy)))
            def _(side=side, lo=lo):
                recv_c[side, :, lo:lo + 4, :] = jnp.zeros((FIELDS, 4, LANES), jnp.float32)

    def clear_unsent(z, carry):
        for k in range(2):
            halo_consts[k, z, 3:5, :] = jnp.zeros((2, COLS), jnp.float32)
        return carry

    lax.fori_loop(0, NZ, clear_unsent, 0)
    for p in range(PORTS):
        for c in range(2):
            own_m[p, c, NZ] = jnp.zeros((ROWS, COLS), jnp.float32)
            halo_m[p, c, NZ] = jnp.zeros((ROWS, COLS), jnp.float32)
    for ref in elecs:
        for c in range(2):
            for rt in (OWN, HALO):
                ref[c, NZ, rt] = jnp.zeros((ROWS, COLS), jnp.float32)

    for load in small_loads:
        load.wait()

    taps = [[], [], [], []]
    for region in range(REGIONS):
        total = [0.0, 0.0, 0.0, 0.0]
        for pole in range(2):
            a, b, c = pole_a[pole, region], pole_b[pole, region], pole_c[pole, region]
            u1 = c
            u2 = a * u1
            u3 = a * u2 + b * u1
            u4 = a * u3 + b * u2
            steps = (u1, u2 - u1, u3 - u2, u4 - u3)
            total = [total[j] + steps[j] for j in range(4)]
        for j in range(4):
            taps[j].append(total[j])

    def make_coefs(eps, region):
        hits = [region == jnp.float32(r) for r in range(REGIONS - 1)]
        result = [-0.25 * eps]
        for j in range(4):
            value = jnp.full((ROWS, LANES), taps[j][REGIONS - 1], jnp.float32)
            for r in range(REGIONS - 1):
                value = jnp.where(hits[r], taps[j][r], value)
            result.append(1.0 - eps * value if j == 0 else eps * value)
        return result

    for load in loads[:4]:
        load.wait()

    for f in range(FIELDS):
        packed[f] = zero

    def prepare(z, carry):
        at_z = (lane >= 8 * z) & (lane < 8 * z + 8)
        for lt in range(2):
            consts[1, z, :, lane_tile(lt)] = ids[z, :, lane_tile(lt)].astype(jnp.float32)
        weight = [mask[z, :, lane_tile(lt)].astype(jnp.float32) for lt in range(2)]
        for f in range(FIELDS):
            if f < 3 * PORTS:
                p, c = f // 3, f % 3
                tiles = []
                for lt in range(2):
                    value = own_m[p, c, z, :, lane_tile(lt)] * weight[lt]
                    own_m[p, c, z, :, lane_tile(lt)] = value
                    tiles.append(value)
            else:
                tiles = [consts[f - 3 * PORTS, z, :, lane_tile(lt)] for lt in range(2)]
            edge = jnp.where(lane < 4, tiles[0], tiles[1])
            packed[f] = jnp.where(at_z, pltpu.roll(edge, lax.rem(8 * z + 4, LANES), 1), packed[f])
        return carry

    lax.fori_loop(0, NZ, prepare, 0)

    peers = 0
    for dx, dy in NEIGHBOURS:
        peers = peers + jnp.where(there(dx, dy), 1, 0)
    pl.semaphore_wait(barrier, peers)

    def remote(index, src, dst, dx, dy):
        return pltpu.make_async_remote_copy(
            src_ref=src, dst_ref=dst, send_sem=send_sem.at[index], recv_sem=recv_sem.at[index],
            device_id=(gx + dx, gy + dy), device_id_type=MESH,
        )

    def rows_of(dx):
        return pl.ds(4, 4) if dx > 0 else pl.ds(0, 4)

    def port_copy(p, dx):
        side = 0 if dx > 0 else 1
        return remote(
            16 + 2 * p + side, own_m.at[p, :, pl.ds(0, NZ), rows_of(dx), :],
            halo_m.at[p, :, pl.ds(0, NZ), rows_of(dx), :], dx, 0,
        )

    edge_copies = []
    for dx, dy in EDGE_ORDER:
        if dy == 0:
            src, dst = packed.at[:, rows_of(dx), :], recv_x.at[:, rows_of(dx), :]
        elif dx == 0:
            src, dst = packed, recv_y.at[0 if dy > 0 else 1]
        else:
            src = packed.at[:, rows_of(dx), :]
            dst = recv_c.at[0 if dy > 0 else 1, :, rows_of(dx), :]
        edge_copies.append((dx, dy, remote(len(edge_copies), src, dst, dx, dy)))
    for dx in (1, -1):
        rows = pl.ds(5, 3) if dx > 0 else pl.ds(0, 3)
        edge_copies.append((dx, 0, remote(
            len(edge_copies), consts.at[:, :, rows, :], halo_consts.at[:, :, rows, :], dx, 0)))

    for dx, dy, copy in edge_copies:
        @pl.when(there(dx, dy))
        def _(copy=copy):
            copy.start()

    def start_port(p):
        for dx in (1, -1):
            @pl.when(there(dx, 0))
            def _(dx=dx):
                port_copy(p, dx).start()

    def sent_port(p):
        for dx in (1, -1):
            @pl.when(there(dx, 0))
            def _(dx=dx):
                port_copy(p, dx).wait_send()

    start_port(0)

    def coef_rows(source, rt):
        def body(z, carry):
            for lt in range(2):
                values = make_coefs(source[0, z, :, lane_tile(lt)], source[1, z, :, lane_tile(lt)])
                for k in range(5):
                    coefs[k, z, rt, :, lane_tile(lt)] = values[k]
            return carry

        lax.fori_loop(0, NZ, body, 0)

    coef_rows(consts, OWN)
    for dx, dy, copy in edge_copies[len(EDGE_ORDER):]:
        @pl.when(there(-dx, -dy))
        def _(copy=copy):
            copy.wait_recv()
    coef_rows(halo_consts, HALO)
    for dx, dy, copy in edge_copies[:len(EDGE_ORDER)]:
        @pl.when(there(-dx, -dy))
        def _(copy=copy):
            copy.wait_recv()
    sent_port(0)
    start_port(1)
    for rt, middle, sides in ((OWN, packed, recv_y), (HALO, recv_x, recv_c)):
        for side in (LEFT, RIGHT):
            def joined(f):
                if side == LEFT:
                    return jnp.where(left_cols, sides[0, f], middle[f])
                return jnp.where(left_cols, middle[f], sides[1, f])

            for f in range(FIELDS - 2):
                strip_m[side, rt, f] = joined(f)
            values = make_coefs(joined(FIELDS - 2), joined(FIELDS - 1))
            for k in range(5):
                strip_coefs[side, rt, k] = values[k]

    def up_row(values):
        rolled = [pltpu.roll(value, ROWS - 1, 0) for value in values]
        return [
            jnp.where(last_row, rolled[1 - rt], rolled[rt]) for rt in (OWN, HALO)
        ]

    def down_row(values):
        rolled = [pltpu.roll(value, 1, 0) for value in values]
        return [
            jnp.where(first_row, rolled[1 - rt], rolled[rt]) for rt in (OWN, HALO)
        ]

    def up_col(tiles, inserted):
        rolled = [pltpu.roll(tile, LANES - 1, 1) for tile in tiles]
        return [
            jnp.where(last_lane, rolled[1], rolled[0]),
            jnp.where(last_lane, inserted, rolled[1]),
        ]

    def up_col_first(tiles, inserted):
        return [
            pltpu.roll(jnp.where(first_lane, tiles[1], tiles[0]), LANES - 1, 1),
            pltpu.roll(jnp.where(first_lane, inserted, tiles[1]), LANES - 1, 1),
        ]

    def down_col(tiles, inserted):
        rolled = [pltpu.roll(tile, 1, 1) for tile in tiles]
        return [
            jnp.where(first_lane, inserted, rolled[0]),
            jnp.where(first_lane, rolled[0], rolled[1]),
        ]

    def down_col_last(tiles, inserted):
        return [
            pltpu.roll(jnp.where(last_lane, inserted, tiles[0]), 1, 1),
            pltpu.roll(jnp.where(last_lane, tiles[0], tiles[1]), 1, 1),
        ]

    both = (OWN, HALO)

    def strip_up_z(value):
        return jnp.where(last_z, 0.0, pltpu.roll(value, LANES - 8, 1))

    def strip_down_z(value):
        return jnp.where(first_z, 0.0, pltpu.roll(value, 8, 1))

    def strip_steps(p):
        amplitude = [waveform[p, plan[s]] for s in range(STEPS)]
        el = [
            [[strip_m[side, rt, 3 * p + c] * amplitude[0] for rt in both] for c in range(3)]
            for side in (LEFT, RIGHT)
        ]
        mags = [None, None]
        sects = [[], []]
        for s in range(STEPS):
            ex, ez = el[RIGHT][0], el[RIGHT][2]
            for rt in both:
                edge_e[p, s, rt] = jnp.where(group == 5, pltpu.roll(ex[rt], 1, 1), ez[rt])
            for side in (LEFT, RIGHT):
                if side == RIGHT and s == STEPS - 1:
                    continue
                ex, ey, ez = el[side]
                ey_up, ez_up = up_row(ey), up_row(ez)
                new = [[None, None] for _ in range(3)]
                for rt in both:
                    curls = (
                        (pltpu.roll(ez[rt], LANES - 1, 1) - ez[rt]) - (strip_up_z(ey[rt]) - ey[rt]),
                        (strip_up_z(ex[rt]) - ex[rt]) - (ez_up[rt] - ez[rt]),
                        (ey_up[rt] - ey[rt]) - (pltpu.roll(ex[rt], LANES - 1, 1) - ex[rt]),
                    )
                    for c in range(3):
                        value = curls[c] if s == 0 else mags[side][c][rt] + curls[c]
                        if c != 1 and side == LEFT:
                            value = jnp.where(keep_low_y, value, 0.0)
                        if c != 0 and rt == HALO:
                            value = jnp.where(keep_low_x, value, 0.0)
                        new[c][rt] = value
                mags[side] = new
                hx, hy, hz = new
                if side == LEFT:
                    for rt in both:
                        edge_h[p, s, rt] = jnp.where(group == 4, pltpu.roll(hz[rt], 1, 1), hx[rt])
                if s == STEPS - 1:
                    continue
                hy_down, hz_down = down_row(hy), down_row(hz)
                sect = [[None, None] for _ in range(3)]
                after = [[None, None] for _ in range(3)]
                for rt in both:
                    backs = (
                        (hz[rt] - pltpu.roll(hz[rt], 1, 1)) - (hy[rt] - strip_down_z(hy[rt])),
                        (hx[rt] - strip_down_z(hx[rt])) - (hz[rt] - hz_down[rt]),
                        (hy[rt] - hy_down[rt]) - (hx[rt] - pltpu.roll(hx[rt], 1, 1)),
                    )
                    for c in range(3):
                        value = el[side][c][rt] + strip_coefs[side, rt, 0] * backs[c]
                        sect[c][rt] = value
                        result = strip_coefs[side, rt, 1] * value
                        for j in range(1, s + 1):
                            result = result - strip_coefs[side, rt, 1 + j] * sects[side][s - j][c][rt]
                        after[c][rt] = result + strip_m[side, rt, 3 * p + c] * amplitude[s + 1]
                sects[side].append(sect)
                el[side] = after

    def cell_pass(p, s, amplitude):
        last = s == STEPS - 1
        elec_in, elec_out = elecs[s % 2], elecs[(s + 1) % 2]
        magn_in, magn_out = magns[(s + 1) % 2], magns[s % 2]
        sources = (own_m, halo_m)

        def read_elec(c, z):
            if s == 0:
                return [[sources[rt][p, c, z, :, lane_tile(lt)] * amplitude[0] for lt in range(2)] for rt in both]
            return [[elec_in[c, z, rt, :, lane_tile(lt)] for lt in range(2)] for rt in both]

        def one_plane(z, el, el_up, mag_down):
            ex, ey, ez = el
            ey_xn = [up_row([ey[rt][lt] for rt in both]) for lt in range(2)]
            ez_xn = [up_row([ez[rt][lt] for rt in both]) for lt in range(2)]
            mags = [[[None] * 2 for _ in both] for _ in range(3)]
            for rt in both:
                inserted = insert_e[p, s, rt, z]
                ex_yn = up_col_first(ex[rt], inserted)
                if not (last and rt == HALO):
                    ez_yn = up_col(ez[rt], inserted)
                for lt in range(2):
                    for c in range(3):
                        if last and rt == HALO and c == 0:
                            continue
                        if c == 0:
                            value = (ez_yn[lt] - ez[rt][lt]) - (el_up[1][rt][lt] - ey[rt][lt])
                        elif c == 1:
                            value = (el_up[0][rt][lt] - ex[rt][lt]) - (ez_xn[lt][rt] - ez[rt][lt])
                        else:
                            value = (ey_xn[lt][rt] - ey[rt][lt]) - (ex_yn[lt] - ex[rt][lt])
                        if s > 0:
                            value = magn_in[c, z, rt, :, lane_tile(lt)] + value
                        if rt == HALO and c != 0:
                            value = jnp.where(keep_low_x, value, 0.0)
                        if not last:
                            magn_out[c, z, rt, :, lane_tile(lt)] = value
                        elif rt == OWN:
                            out_h[p, c, z, :, lane_tile(lt)] = -0.5 * value
                        mags[c][rt][lt] = value
            hx, hy, hz = mags
            hy_xp = [down_row([hy[rt][lt] for rt in both]) for lt in range(2)]
            hz_xp = [down_row([hz[rt][lt] for rt in both]) for lt in range(2)]
            for rt in both:
                if last and rt == HALO:
                    continue
                inserted = insert_h[p, s, rt, z]
                hx_yp = down_col_last(hx[rt], inserted)
                hz_yp = down_col(hz[rt], inserted)
                for lt in range(2):
                    hx_zp, hy_zp = mag_down[0][rt][lt], mag_down[1][rt][lt]
                    backs = (
                        (hz[rt][lt] - hz_yp[lt]) - (hy[rt][lt] - hy_zp),
                        (hx[rt][lt] - hx_zp) - (hz[rt][lt] - hz_xp[lt][rt]),
                        (hy[rt][lt] - hy_xp[lt][rt]) - (hx[rt][lt] - hx_yp[lt]),
                    )
                    factors = [coefs[k, z, rt, :, lane_tile(lt)] for k in range(2 + s)]
                    for c in range(3):
                        value = el[c][rt][lt] + factors[0] * backs[c]
                        new = factors[1] * value
                        for j in range(1, s + 1):
                            new = new - factors[1 + j] * sects[s - j][c, z, rt, :, lane_tile(lt)]
                        if last:
                            out_e[p, c, z, :, lane_tile(lt)] = new
                            continue
                        new = new + sources[rt][p, c, z, :, lane_tile(lt)] * amplitude[s + 1]
                        sects[s][c, z, rt, :, lane_tile(lt)] = value
                        elec_out[c, z, rt, :, lane_tile(lt)] = new
            return mags

        nothing = (zero, zero)
        kept = (OWN,) if last else both

        def body(block, carry):
            mags = [[list(carry[c][rt]) if rt in kept else nothing for rt in both] for c in range(2)]
            first = block * UNROLL
            el = [read_elec(c, first) for c in range(3)]
            for offset in range(UNROLL):
                last_offset = offset == UNROLL - 1
                el_up = [read_elec(c, first + offset + 1) for c in range(2 if last_offset else 3)]
                mags = one_plane(first + offset, el, el_up, mags)
                el = el_up
            return tuple(tuple(tuple(mags[c][rt]) for rt in kept) for c in range(2))

        lax.fori_loop(0, NZ // UNROLL, body, ((nothing,) * len(kept),) * 2)

    def strips(block, carry):
        for offset in range(2):
            strip_steps(2 * block + offset)
        return carry

    def place(p, carry):
        for s in range(STEPS):
            for rt in both:
                value_e, value_h = edge_e[p, s, rt], edge_h[p, s, rt]
                for z in range(NZ):
                    insert_e[p, s, rt, z] = pltpu.roll(value_e, (251 - 8 * z) % LANES, 1)
                    if rt == OWN or s < STEPS - 1:
                        insert_h[p, s, rt, z] = pltpu.roll(value_h, (252 - 8 * z) % LANES, 1)
        return carry

    lax.fori_loop(0, PORTS // 2, strips, 0)
    lax.fori_loop(0, PORTS, place, 0)
    sent_port(1)
    start_port(2)

    def port_body(p, carry):
        amplitude = [waveform[p, plan[s]] for s in range(STEPS)]
        for dx in (1, -1):
            @pl.when(there(-dx, 0))
            def _(dx=dx):
                port_copy(p, dx).wait_recv()

        for s in range(STEPS):
            if s == 1:
                @pl.when(p == 0)
                def _():
                    sent_port(2)
                    start_port(3)

            cell_pass(p, s, amplitude)
        return carry

    lax.fori_loop(0, PORTS, port_body, 0)

    for dx, dy, copy in edge_copies:
        @pl.when(there(dx, dy))
        def _(copy=copy):
            copy.wait_send()
    sent_port(PORTS - 1)


def local(residual, eps_inv, region_ids, source_mask, pole_a, pole_b, pole_c, waveform, plan):
    hbm = pl.BlockSpec(memory_space=pl.ANY)
    vmem = pl.BlockSpec(memory_space=pltpu.VMEM)
    shape = (PORTS, 3, NZ, ROWS, COLS)
    f32 = jnp.float32
    return pl.pallas_call(
        kernel,
        out_shape=[jax.ShapeDtypeStruct(shape, f32)] * 2,
        in_specs=[hbm] * 9,
        out_specs=[vmem] * 2,
        scratch_shapes=[
            *[pltpu.SMEM((2, REGIONS), f32)] * 3,
            pltpu.SMEM((PORTS, waveform.shape[0]), f32),
            pltpu.SMEM((STEPS,), jnp.int32),
            *[pltpu.VMEM((PORTS, 3, NZ + 1, ROWS, COLS), f32)] * 2,
            pltpu.VMEM((NZ, ROWS, COLS), jnp.int32),
            pltpu.VMEM((NZ, ROWS, COLS), jnp.int32),
            pltpu.VMEM((2, NZ, ROWS, COLS), f32),
            pltpu.VMEM((2, NZ, ROWS, COLS), f32),
            pltpu.VMEM((FIELDS, ROWS, LANES), f32),
            pltpu.VMEM((FIELDS, ROWS, LANES), f32),
            pltpu.VMEM((2, FIELDS, ROWS, LANES), f32),
            pltpu.VMEM((2, FIELDS, ROWS, LANES), f32),
            *[pltpu.VMEM((3, NZ + 1, 2, ROWS, COLS), f32)] * 2,
            *[pltpu.VMEM((3, NZ, 2, ROWS, COLS), f32)] * 5,
            pltpu.VMEM((5, NZ, 2, ROWS, COLS), f32),
            pltpu.VMEM((2, 2, 3 * PORTS, ROWS, LANES), f32),
            pltpu.VMEM((2, 2, 5, ROWS, LANES), f32),
            *[pltpu.VMEM((PORTS, STEPS, 2, ROWS, LANES), f32)] * 2,
            *[pltpu.VMEM((PORTS, STEPS, 2, NZ, ROWS, LANES), f32)] * 2,
            pltpu.SemaphoreType.DMA((9,)),
            pltpu.SemaphoreType.DMA((16 + 2 * PORTS,)),
            pltpu.SemaphoreType.DMA((16 + 2 * PORTS,)),
        ],
        compiler_params=pltpu.CompilerParams(
            collective_id=0, has_side_effects=True, vmem_limit_bytes=40 << 20
        ),
        cost_estimate=pl.CostEstimate(flops=60000000, bytes_accessed=5242880, transcendentals=0),
    )(*[
        pltpu.with_memory_space_constraint(value, pltpu.HBM)
        for value in (
            residual, eps_inv, region_ids, source_mask, pole_a.T, pole_b.T, pole_c.T, waveform.T, plan
        )
    ])


def solution(mesh):
    cells = P(None, "gx", "gy")
    fields = P(None, None, None, "gx", "gy")
    return jax.shard_map(
        local,
        mesh=mesh,
        in_specs=(fields, cells, cells, cells, P(), P(), P(), P(), P()),
        out_specs=(fields, fields),
        check_vma=False,
    )
```
